32 devices in a mesh: parts: 2 (over y), seq: 4 (over z), fsdp: 2 (over x), chan: 2 (over core).
Axes of the slice: x: 2, y: 2, z: 4, core: 2. Of those that a mesh axis runs over, the one named last changes fastest.
Arguments:
- ids: int32 [3072], P(('parts', 'seq')), parts along dimension 0, may hold values from 0 to 511
- embed: bfloat16 [512, 4096], replicated, may hold values from -6 to 6
- norm_gain: float32 [4096], replicated, may hold values from 0.1 to 1.9
- w_in: bfloat16 [4096, 3, 4096], P('seq', None, ('fsdp', 'chan')), may hold values from -0.09375 to 0.09375
- short_filter: float32 [3, 3, 4096], P(None, None, ('fsdp', 'chan')), may hold values from -3 to 3
- long_filter: float32 [256, 128], P(('fsdp', 'chan')), may hold values from -1 to 1
- skip_bias: float32 [4096], P(('fsdp', 'chan')), may hold values from -4 to 4
- w_out: bfloat16 [4096, 4096], P('seq', ('fsdp', 'chan')), may hold values from -0.09375 to 0.09375
Outputs:
- block_out: bfloat16 [3072, 4096], P(('parts', 'seq'), ('fsdp', 'chan')), parts along dimension 0
The draws below stay inside these ranges and needn't reach their ends.
There are 2 independent parts, one for each index of `parts`. The reference program is written for one: setup_inputs(seed, part) draws one part's arguments, and reference() takes and returns one part's arrays. A program takes and returns all parts, laid end to end along the dimension named above; an argument that names none is the same for every part. Nothing has to cross between parts.
All inputs are finite; a program needn't handle non-finite values.
Results may differ from the reference program's by a relative error of at most 0.0082.
Values may be sent and summed in bfloat16 or wider, within the bound.
No kernel may reach another device: no remote copies, remote signals or barrier semaphores. Data moves between devices by JAX's collectives and lax.ppermute only.
A program may use at most 128 MiB of HBM per device.

```python
import math
import jax
import jax.numpy as jnp
import numpy as np
from jax import lax

D = 4096
GROUPS = 256
FL = 128
SHORT = 3
VOCAB = 512
SEQ_LEN = 1536


def touch_ends(array, rng, least, high):
    extent = array.shape
    place = [jax.random.randint(jax.random.fold_in(rng, axis), (), 0, extent[axis]) for axis in range(len(extent))]
    array = array.at[tuple(place)].set(least)
    longest = extent.index(max(extent))
    place[longest] = (place[longest] + 1) % extent[longest]
    return array.at[tuple(place)].set(high)


def level_of(stream_key, shape, pieces, least, high):
    level, own = 1.0, jax.random.fold_in(stream_key, 6)
    for dim, blocks in pieces:
        steps = jnp.exp(jax.random.uniform(jax.random.fold_in(own, dim), (blocks,), jnp.float32, least / len(pieces), high / len(pieces)))
        level = level * jnp.repeat(steps, shape[dim] // blocks).reshape([-1 if axis == dim else 1 for axis in range(len(shape))])
    return level


def cumulative_ranks(count, slope):
    weights = [(1 << 20) // math.isqrt(grade ** slope) + 1 for grade in range(1, count + 1)]
    width = 1 + sum(weights) // (1 << 30)
    return np.cumsum(np.array([max(1, weight // width) for weight in weights]))


def ranked(rng, dims, number_of, lean):
    listing = cumulative_ranks(number_of, lean)
    lot = jax.random.randint(jax.random.fold_in(rng, 1), dims, 0, int(listing[number_of - 1]))
    rank = jnp.searchsorted(jnp.asarray(listing, jnp.int32), lot, side="right")
    return jax.random.permutation(jax.random.fold_in(rng, 2), number_of)[rank].astype(jnp.int32)


def bell_draw(own_key, shape, deviation, bound, split=(), kind=jnp.bfloat16):
    result = deviation * jax.random.normal(own_key, shape, jnp.float32)
    if split:
        result = result * level_of(own_key, shape, split, -0.22, 0.18)
    return jnp.clip(result, -bound, bound).astype(kind)


def setup_inputs(seed: int = 0, part: int = 0) -> dict:
    seeds = jax.random.split(jax.random.key(seed), 9)
    part_splits = jax.random.split(jax.random.fold_in(seeds[8], part), 9)
    return {
        "ids": touch_ends(ranked(part_splits[0], (SEQ_LEN,), VOCAB, 2), jax.random.fold_in(part_splits[0], 3), 0, VOCAB - 1).astype(jnp.int32),
        "embed": bell_draw(seeds[1], (VOCAB, D), 1.0, 6.0),
        "norm_gain": jnp.clip(1.0 + 0.18 * jax.random.normal(seeds[2], (D,), jnp.float32), 0.1, 1.9),
        "w_in": bell_draw(seeds[3], (D, 3, D), D ** -0.5, 0.09375, ((0, 4), (2, 4))),
        "short_filter": bell_draw(seeds[4], (SHORT, 3, D), 0.6, 3.0, ((2, 4),), jnp.float32),
        "long_filter": bell_draw(seeds[5], (GROUPS, FL), 0.15, 1.0, ((0, 4),), jnp.float32),
        "skip_bias": bell_draw(seeds[6], (D,), 1.0, 4.0, ((0, 4),), jnp.float32),
        "w_out": bell_draw(seeds[7], (D, D), D ** -0.5, 0.09375, ((0, 4), (1, 4))),
    }


def reference(ids, embed, norm_gain, w_in, short_filter, long_filter, skip_bias, w_out):
    embedded = embed[ids]
    values = embedded.astype(jnp.float32)
    scaled = values * lax.rsqrt(lax.optimization_barrier(jnp.mean(values * values, axis=1, keepdims=True)) + 1e-06) * norm_gain
    normed = scaled.astype(jnp.bfloat16)
    projected = jnp.dot(normed, w_in.reshape(D, 3 * D), preferred_element_type=jnp.float32)
    projected = projected.astype(jnp.bfloat16).reshape(SEQ_LEN, 3, D)
    padded = jnp.concatenate([jnp.zeros((SHORT - 1, 3, D), jnp.float32), projected.astype(jnp.float32)], axis=0)
    mixed = jnp.zeros((SEQ_LEN, 3, D), jnp.float32)
    for offset in range(SHORT):
        mixed = mixed + short_filter[offset] * padded[SHORT - 1 - offset:SHORT - 1 - offset + SEQ_LEN]
    product = (mixed[:, 1, :] * mixed[:, 2, :]).astype(jnp.bfloat16)
    per_channel = jnp.repeat(long_filter, D // GROUPS, axis=0)
    upadded = jnp.concatenate([jnp.zeros((FL - 1, D), jnp.float32), product.astype(jnp.float32)], axis=0)

    def one_tap(offset, total):
        column = lax.dynamic_slice_in_dim(per_channel, offset, 1, 1)[:, 0]
        return total + column * lax.dynamic_slice_in_dim(upadded, FL - 1 - offset, SEQ_LEN, 0)
    conv = lax.fori_loop(0, FL, one_tap, jnp.zeros((SEQ_LEN, D), jnp.float32))
    gated = (mixed[:, 0, :] * (conv + skip_bias * product.astype(jnp.float32))).astype(jnp.bfloat16)
    update = jnp.dot(gated, w_out, preferred_element_type=jnp.float32)
    return (values + update).astype(jnp.bfloat16)
```

```python
import functools

import jax
import jax.numpy as jnp
from jax import lax
from jax.experimental import pallas as pl
from jax.experimental.pallas import tpu as pltpu
from jax.sharding import PartitionSpec as P

FL = 128
SHORT = 3
VMEM = 56 * 1024 * 1024


def moved(value, axis, steps):
    count = lax.axis_size(axis)
    return lax.ppermute(value, axis, [(source, (source + steps) % count) for source in range(count)])


def project_kernel(where, rows, cut, gain, w, out, normed):
    seqs = out.shape[0]
    mine = out.shape[1] // 3
    branch = pl.program_id(0)

    @pl.when(branch == 0)
    def _():
        values = rows[...].astype(jnp.float32)
        scale = lax.rsqrt(jnp.mean(values * values, axis=1, keepdims=True) + 1e-06)
        normed[...] = (cut[...].astype(jnp.float32) * scale * gain[...]).astype(jnp.bfloat16)

    partial = jnp.dot(normed[...], w[0], preferred_element_type=jnp.float32)
    turned = partial.T.astype(jnp.bfloat16)
    for dest in range(seqs):
        slot = lax.rem(dest - where[1] + seqs, seqs)
        out[slot, pl.ds(branch * mine, mine), :] = turned[dest * mine : (dest + 1) * mine]


def project(where, embed, gain, w, seqs, parts):
    branches, depth, chans = w.shape
    rows = embed.shape[0] // parts
    mine = chans // seqs
    width = embed.shape[1]
    return pl.pallas_call(
        project_kernel,
        grid_spec=pltpu.PrefetchScalarGridSpec(
            num_scalar_prefetch=1,
            grid=(branches,),
            in_specs=[
                pl.BlockSpec((rows, width), lambda i, at: (at[0], 0)),
                pl.BlockSpec((rows, depth), lambda i, at: (at[0], at[1])),
                pl.BlockSpec((1, depth), lambda i, at: (0, at[1])),
                pl.BlockSpec((1, depth, chans), lambda i, at: (i, 0, 0)),
            ],
            out_specs=pl.BlockSpec((seqs, branches * mine, rows), lambda i, at: (0, 0, 0)),
            scratch_shapes=[pltpu.VMEM((rows, depth), jnp.bfloat16)],
        ),
        out_shape=jax.ShapeDtypeStruct((seqs, branches * mine, rows), jnp.bfloat16),
        compiler_params=pltpu.CompilerParams(vmem_limit_bytes=VMEM),
        cost_estimate=pl.CostEstimate(
            flops=2 * rows * depth * chans * branches,
            bytes_accessed=2 * (rows * width + depth * chans * branches),
            transcendentals=0,
        ),
    )(where, embed, embed, gain, w)


def bands_kernel(taps, out):
    groups = taps.shape[0]
    for group in range(groups):
        line = jnp.concatenate([taps[group : group + 1, :], jnp.zeros((1, FL), jnp.float32)], axis=1)
        wide = jnp.broadcast_to(line, (2 * FL, 2 * FL))
        band = pltpu.roll(wide, FL, 1, stride=1, stride_axis=0)[:, :FL]
        high = band.astype(jnp.bfloat16)
        low = (band - high.astype(jnp.float32)).astype(jnp.bfloat16)
        out[group] = jnp.concatenate([high, low], axis=1)


def bands_of(taps):
    groups = taps.shape[0]
    return pl.pallas_call(
        bands_kernel,
        out_shape=jax.ShapeDtypeStruct((groups, 2 * FL, 2 * FL), jnp.bfloat16),
        compiler_params=pltpu.CompilerParams(vmem_limit_bytes=VMEM),
    )(taps)


def mixing_kernel(per_group, parts, where, *refs):
    tables, (hot, factors, bands, out, wide, gated) = refs[:parts], refs[parts:]
    seqs, held, lanes = out.shape
    tokens = hot.shape[1]
    blocks = tokens // FL
    rows = tables[0].shape[2]
    for branch in range(3):
        total = None
        for piece in range(parts):
            term = jnp.dot(
                tables[piece][branch],
                hot[piece * rows : (piece + 1) * rows, :],
                preferred_element_type=jnp.float32,
            )
            total = term if total is None else total + term
        wide[branch] = total
    place = lax.broadcasted_iota(jnp.int32, (per_group, tokens), 1)
    for group in range(lanes // per_group):
        at = slice(group * per_group, (group + 1) * per_group)

        def mixed(branch):
            now = wide[branch, at, :]
            total = factors[at, branch : branch + 1] * now
            for offset in range(1, SHORT):
                before = jnp.where(place >= offset, pltpu.roll(now, offset, 1), 0.0)
                column = 3 * offset + branch
                total = total + factors[at, column : column + 1] * before
            return total

        product = (mixed(1) * mixed(2)).astype(jnp.bfloat16)
        past = jnp.concatenate([jnp.zeros((per_group, FL), jnp.bfloat16), product[:, :-FL]], axis=1)
        windows = jnp.concatenate(
            [
                jnp.concatenate([past[:, b * FL : (b + 1) * FL], product[:, b * FL : (b + 1) * FL]], axis=1)
                for b in range(blocks)
            ],
            axis=0,
        )
        both = jnp.dot(windows, bands[group], preferred_element_type=jnp.float32)
        summed = both[:, :FL] + both[:, FL:]
        conv = jnp.concatenate([summed[b * per_group : (b + 1) * per_group] for b in range(blocks)], axis=1)
        skip = factors[at, 3 * SHORT : 3 * SHORT + 1]
        gated[at, :] = mixed(0) * (conv + skip * product.astype(jnp.float32))
    for dest in range(seqs):
        slot = lax.rem(dest - where[1] + seqs, seqs)
        part = gated[:, dest * held : (dest + 1) * held]
        out[slot] = part.T.astype(jnp.bfloat16)


def mixing(where, tables, hot, factors, bands, seqs):
    _, mine, rows = tables[0].shape
    parts = len(tables)
    tokens = hot.shape[1]
    groups = bands.shape[0]
    per_group = mine // groups
    step = min(mine, FL)
    held = tokens // seqs
    return pl.pallas_call(
        functools.partial(mixing_kernel, per_group, parts),
        grid_spec=pltpu.PrefetchScalarGridSpec(
            num_scalar_prefetch=1,
            grid=(mine // step,),
            in_specs=[pl.BlockSpec((3, step, rows), lambda i, at: (0, i, 0))] * parts
            + [
                pl.BlockSpec(hot.shape, lambda i, at: (0, 0)),
                pl.BlockSpec((step, factors.shape[1]), lambda i, at: (i, 0)),
                pl.BlockSpec((step // per_group, 2 * FL, 2 * FL), lambda i, at: (i, 0, 0)),
            ],
            out_specs=pl.BlockSpec((seqs, held, step), lambda i, at: (0, 0, i)),
            scratch_shapes=[
                pltpu.VMEM((3, step, tokens), jnp.float32),
                pltpu.VMEM((step, tokens), jnp.float32),
            ],
        ),
        out_shape=jax.ShapeDtypeStruct((seqs, held, mine), jnp.bfloat16),
        compiler_params=pltpu.CompilerParams(vmem_limit_bytes=VMEM),
        cost_estimate=pl.CostEstimate(
            flops=2 * 3 * mine * rows * parts * tokens,
            bytes_accessed=2 * hot.size,
            transcendentals=0,
        ),
    )(where, *tables, hot, factors, bands)


def on_device(ids, embed, norm_gain, w_in, short_filter, long_filter, skip_bias, w_out):
    held = ids.shape[0]
    chans = skip_bias.shape[0]
    vocab = embed.shape[0]
    seqs, parts = lax.axis_size("seq"), lax.axis_size("parts")
    fsdps, cores = lax.axis_size("fsdp"), lax.axis_size("chan")
    seq, part = lax.axis_index("seq"), lax.axis_index("parts")
    mine = chans // seqs
    rows = vocab // parts
    where = jnp.stack([part, seq]).astype(jnp.int32)

    depth = w_out.shape[0]
    share = depth // parts
    ring = lax.dynamic_slice_in_dim(w_out, part * share, share, 0)
    whole = jnp.zeros((seqs * depth, chans), w_out.dtype)
    whole = lax.dynamic_update_slice_in_dim(whole, w_out, seq * depth, 0)
    for hop in range(1, seqs):
        ring = moved(ring, "seq", 1)
        owner = lax.rem(seq - hop + seqs, seqs)
        whole = lax.dynamic_update_slice_in_dim(whole, ring, owner * depth + part * share, 0)
        for across in range(1, parts):
            other = moved(ring, "parts", across)
            source = lax.rem(part - across + parts, parts)
            whole = lax.dynamic_update_slice_in_dim(whole, other, owner * depth + source * share, 0)

    slots = project(where, embed, norm_gain[None, :], w_in.transpose(1, 0, 2), seqs, parts)
    total = slots[0].astype(jnp.float32)
    for hop in range(1, seqs):
        total = total + moved(slots[hop], "seq", hop).astype(jnp.float32)
    table = total.astype(jnp.bfloat16).reshape(3, mine, rows)
    tables = [table] + [moved(table, "parts", across) for across in range(1, parts)]

    every_id = lax.all_gather(ids, "seq", axis=0, tiled=True)
    place = lax.broadcasted_iota(jnp.int32, (parts, rows, 1), 1)
    order = lax.broadcasted_iota(jnp.int32, (parts, rows, 1), 0)
    place = place + lax.rem(part - order + parts, parts) * rows
    hot = (place.reshape(vocab, 1) == every_id[None, :]).astype(jnp.bfloat16)

    first = seq * mine
    short = lax.dynamic_slice_in_dim(short_filter.reshape(3 * SHORT, chans), first, mine, 1)
    skip = lax.dynamic_slice_in_dim(skip_bias, first, mine, 0)
    factors = jnp.concatenate([short, skip[None, :], jnp.zeros((6, mine), jnp.float32)], axis=0).T
    groups = long_filter.shape[0] // seqs
    bands = bands_of(lax.dynamic_slice_in_dim(long_filter, seq * groups, groups, 0))
    sends = mixing(where, tables, hot, factors, bands, seqs)

    gated = jnp.zeros((held, seqs, mine), jnp.bfloat16)
    for hop in range(seqs):
        piece = sends[0] if hop == 0 else moved(sends[hop], "seq", hop)
        owner = lax.rem(seq - hop + seqs, seqs)
        gated = lax.dynamic_update_slice(gated, piece[:, None, :], (0, owner, 0))
    gated = gated.reshape(held, chans)
    fsdp, core = lax.axis_index("fsdp"), lax.axis_index("chan")
    columns = jnp.zeros((held, fsdps * cores * chans), jnp.bfloat16)
    for across in range(fsdps):
        near = gated if across == 0 else moved(gated, "fsdp", across)
        x = lax.rem(fsdp - across + fsdps, fsdps)
        for turn in range(cores):
            piece = near if turn == 0 else moved(near, "chan", turn)
            c = lax.rem(core - turn + cores, cores)
            columns = lax.dynamic_update_slice(columns, piece, (0, (x * cores + c) * chans))

    update = jnp.dot(columns, whole, preferred_element_type=jnp.float32)
    position = lax.axis_index(("fsdp", "chan"))
    onehot = (ids[:, None] == lax.broadcasted_iota(jnp.int32, (1, vocab), 1)).astype(jnp.bfloat16)
    residual = jnp.dot(
        onehot,
        lax.dynamic_slice_in_dim(embed, position * chans, chans, 1),
        preferred_element_type=jnp.float32,
    )
    return (residual + update).astype(jnp.bfloat16)


def solution(mesh):
    in_specs = (
        P(("parts", "seq")),
        P(),
        P(),
        P("seq", None, ("fsdp", "chan")),
        P(None, None, ("fsdp", "chan")),
        P(("fsdp", "chan"), None),
        P(("fsdp", "chan")),
        P("seq", ("fsdp", "chan")),
    )
    out_specs = P(("parts", "seq"), ("fsdp", "chan"))
    return jax.shard_map(
        on_device, mesh=mesh, in_specs=in_specs, out_specs=out_specs, check_vma=False
    )
```

```python
import functools

import jax
import jax.numpy as jnp
from jax import lax
from jax.experimental import pallas as pl
from jax.experimental.pallas import tpu as pltpu
from jax.sharding import PartitionSpec as P

FL = 128
SHORT = 3
VMEM = 28 * 1024 * 1024


def moved(value, axis, steps):
    count = lax.axis_size(axis)
    return lax.ppermute(value, axis, [(source, (source + steps) % count) for source in range(count)])


def swapped(value, axis, bits):
    count = lax.axis_size(axis)
    return lax.ppermute(value, axis, [(source, source ^ bits) for source in range(count)])


def after(value, *others):
    return lax.optimization_barrier((value,) + others)[0]


def project_kernel(where, rows, cut, gain, w, *refs):
    outs, (normed, turned) = refs[:-2], refs[-2:]
    seqs = len(outs)
    mine = outs[0].shape[0] // 3
    branch = pl.program_id(0)

    @pl.when(branch == 0)
    def _():
        values = rows[...].astype(jnp.float32)
        scale = lax.rsqrt(jnp.mean(values * values, axis=1, keepdims=True) + 1e-06)
        normed[...] = (cut[...].astype(jnp.float32) * scale * gain[...]).astype(jnp.bfloat16)

    turned[...] = jnp.dot(normed[...], w[0], preferred_element_type=jnp.float32).T
    for slot in range(seqs):
        dest = where[1] ^ slot
        piece = turned[pl.ds(pl.multiple_of(dest * mine, mine), mine), :]
        outs[slot][pl.ds(pl.multiple_of(branch * mine, mine), mine), :] = piece.astype(outs[slot].dtype)


def project(where, embed, gain, w, seqs, parts):
    branches, depth, chans = w.shape
    rows = embed.shape[0] // parts
    mine = chans // seqs
    width = embed.shape[1]
    kinds = [jnp.float32] + [jnp.bfloat16] * (seqs - 1)
    return pl.pallas_call(
        project_kernel,
        grid_spec=pltpu.PrefetchScalarGridSpec(
            num_scalar_prefetch=1,
            grid=(branches,),
            in_specs=[
                pl.BlockSpec((rows, width), lambda i, at: (at[0], 0)),
                pl.BlockSpec((rows, depth), lambda i, at: (at[0], at[1])),
                pl.BlockSpec((1, depth), lambda i, at: (0, at[1])),
                pl.BlockSpec((1, depth, chans), lambda i, at: (i, 0, 0)),
            ],
            out_specs=[pl.BlockSpec((branches * mine, rows), lambda i, at: (0, 0))] * seqs,
            scratch_shapes=[pltpu.VMEM((rows, depth), jnp.bfloat16), pltpu.VMEM((chans, rows), jnp.float32)],
        ),
        out_shape=[jax.ShapeDtypeStruct((branches * mine, rows), kind) for kind in kinds],
        compiler_params=pltpu.CompilerParams(vmem_limit_bytes=VMEM),
        cost_estimate=pl.CostEstimate(
            flops=2 * rows * depth * chans * branches,
            bytes_accessed=2 * (rows * width + depth * chans * branches),
            transcendentals=0,
        ),
    )(where, embed, embed, gain, w)


def bands_kernel(taps, out):
    groups = taps.shape[0]
    for group in range(groups):
        line = jnp.concatenate([taps[group : group + 1, :], jnp.zeros((1, FL), jnp.float32)], axis=1)
        wide = jnp.broadcast_to(line, (2 * FL, 2 * FL))
        band = pltpu.roll(wide, FL, 1, stride=1, stride_axis=0)[:, :FL]
        high = band.astype(jnp.bfloat16)
        low = (band - high.astype(jnp.float32)).astype(jnp.bfloat16)
        out[group] = jnp.concatenate([high, low], axis=1)


def bands_of(taps):
    groups = taps.shape[0]
    return pl.pallas_call(
        bands_kernel,
        out_shape=jax.ShapeDtypeStruct((groups, 2 * FL, 2 * FL), jnp.bfloat16),
        compiler_params=pltpu.CompilerParams(vmem_limit_bytes=VMEM),
    )(taps)


def mixing_kernel(per_group, parts, where, *refs):
    tables, (hot, factors, bands), rest = refs[:parts], refs[parts : parts + 3], refs[parts + 3 :]
    outs, (wide, gated) = rest[:-2], rest[-2:]
    seqs = len(outs)
    lanes, held = outs[0].shape
    tokens = hot.shape[1]
    blocks = tokens // FL
    rows = tables[0].shape[2]
    for branch in range(3):
        total = None
        for piece in range(parts):
            term = jnp.dot(
                tables[piece][branch],
                hot[piece * rows : (piece + 1) * rows, :],
                preferred_element_type=jnp.float32,
            )
            total = term if total is None else total + term
        wide[branch] = total
    place = lax.broadcasted_iota(jnp.int32, (per_group, tokens), 1)
    for group in range(lanes // per_group):
        at = slice(group * per_group, (group + 1) * per_group)

        def mixed(branch):
            now = wide[branch, at, :]
            total = factors[at, branch : branch + 1] * now
            for offset in range(1, SHORT):
                before = jnp.where(place >= offset, pltpu.roll(now, offset, 1), 0.0)
                column = 3 * offset + branch
                total = total + factors[at, column : column + 1] * before
            return total

        product = (mixed(1) * mixed(2)).astype(jnp.bfloat16)
        past = jnp.concatenate([jnp.zeros((per_group, FL), jnp.bfloat16), product[:, :-FL]], axis=1)
        windows = jnp.concatenate(
            [
                jnp.concatenate([past[:, b * FL : (b + 1) * FL], product[:, b * FL : (b + 1) * FL]], axis=1)
                for b in range(blocks)
            ],
            axis=0,
        )
        both = jnp.dot(windows, bands[group], preferred_element_type=jnp.float32)
        summed = both[:, :FL] + both[:, FL:]
        conv = jnp.concatenate([summed[b * per_group : (b + 1) * per_group] for b in range(blocks)], axis=1)
        skip = factors[at, 3 * SHORT : 3 * SHORT + 1]
        gated[at, :] = mixed(0) * (conv + skip * product.astype(jnp.float32))
    for slot in range(seqs):
        dest = where[1] ^ slot
        outs[slot][...] = gated[:, pl.ds(pl.multiple_of(dest * held, FL), held)].astype(jnp.bfloat16)


def mixing(where, tables, hot, factors, bands, seqs):
    _, mine, rows = tables[0].shape
    parts = len(tables)
    tokens = hot.shape[1]
    groups = bands.shape[0]
    per_group = mine // groups
    step = min(mine, FL)
    held = tokens // seqs
    return pl.pallas_call(
        functools.partial(mixing_kernel, per_group, parts),
        grid_spec=pltpu.PrefetchScalarGridSpec(
            num_scalar_prefetch=1,
            grid=(mine // step,),
            in_specs=[pl.BlockSpec((3, step, rows), lambda i, at: (0, i, 0))] * parts
            + [
                pl.BlockSpec(hot.shape, lambda i, at: (0, 0)),
                pl.BlockSpec((step, factors.shape[1]), lambda i, at: (i, 0)),
                pl.BlockSpec((step // per_group, 2 * FL, 2 * FL), lambda i, at: (i, 0, 0)),
            ],
            out_specs=[pl.BlockSpec((step, held), lambda i, at: (i, 0))] * seqs,
            scratch_shapes=[
                pltpu.VMEM((3, step, tokens), jnp.float32),
                pltpu.VMEM((step, tokens), jnp.float32),
            ],
        ),
        out_shape=[jax.ShapeDtypeStruct((mine, held), jnp.bfloat16)] * seqs,
        compiler_params=pltpu.CompilerParams(vmem_limit_bytes=VMEM),
        cost_estimate=pl.CostEstimate(
            flops=2 * 3 * mine * rows * parts * tokens,
            bytes_accessed=2 * hot.size,
            transcendentals=0,
        ),
    )(where, *tables, hot, factors, bands)


def output_kernel(axes, stacks, layout, where, *refs):
    parts, seqs, fsdps, cores, depth = axes
    start, arrived, refs = refs[0], refs[1 : 1 + stacks], refs[1 + stacks :]
    pieces, (out, gated, total) = refs[: len(layout)], refs[len(layout) :]
    part, seq, fsdp, core = where[0], where[1], where[2], where[3]
    chans = total.shape[1]
    mine = chans // seqs
    for across in range(fsdps):
        for turn in range(cores):
            block = lax.rem(fsdp - across + fsdps, fsdps) * cores + lax.rem(core - turn + cores, cores)
            for hop in range(seqs):
                row = block * chans + (seq ^ hop) * mine
                piece = arrived[across * cores + turn][hop * mine : (hop + 1) * mine, :]
                gated[pl.ds(pl.multiple_of(row, mine), mine), :] = piece
    for index, (piece, (hop, across, first)) in enumerate(zip(pieces, layout)):
        size = piece.shape[0]
        row = lax.rem(seq - hop + seqs, seqs) * depth + first
        if hop:
            row = row + lax.rem(part - across + parts, parts) * (depth // parts)
        term = lax.dot_general(
            gated[pl.ds(pl.multiple_of(row, size), size), :],
            piece[...],
            (((0,), (0,)), ((), ())),
            preferred_element_type=jnp.float32,
        )
        term = term + (total[...] if index else start[...])
        if index == len(layout) - 1:
            out[...] = term.astype(out.dtype)
        else:
            total[...] = term


def output(axes, where, start, stacks, pieces, layout, kind):
    parts, seqs, fsdps, cores, depth = axes
    held, chans = start.shape
    size = sum(piece.shape[0] for piece in pieces)
    local = pl.BlockSpec(memory_space=pltpu.VMEM)
    return pl.pallas_call(
        functools.partial(output_kernel, axes, len(stacks), tuple(layout)),
        in_specs=[pl.BlockSpec(memory_space=pltpu.SMEM)] + [local] * (1 + len(stacks) + len(pieces)),
        out_specs=local,
        scratch_shapes=[
            pltpu.VMEM((seqs * depth, held), jnp.bfloat16),
            pltpu.VMEM((held, chans), jnp.float32),
        ],
        out_shape=jax.ShapeDtypeStruct((held, chans), kind),
        compiler_params=pltpu.CompilerParams(vmem_limit_bytes=VMEM),
        cost_estimate=pl.CostEstimate(
            flops=2 * held * size * chans, bytes_accessed=2 * size * chans, transcendentals=0
        ),
    )(where, start, *stacks, *pieces)


def on_device(ids, embed, norm_gain, w_in, short_filter, long_filter, skip_bias, w_out):
    held = ids.shape[0]
    chans = skip_bias.shape[0]
    vocab = embed.shape[0]
    seqs, parts = lax.axis_size("seq"), lax.axis_size("parts")
    fsdps, cores = lax.axis_size("fsdp"), lax.axis_size("chan")
    seq, part = lax.axis_index("seq"), lax.axis_index("parts")
    fsdp, core = lax.axis_index("fsdp"), lax.axis_index("chan")
    mine = chans // seqs
    rows = vocab // parts
    depth = w_out.shape[0]
    share = depth // parts
    cuts = 1
    cut = share // cuts
    where = jnp.stack([part, seq, fsdp, core]).astype(jnp.int32)

    rings = [[lax.dynamic_slice_in_dim(w_out, part * share + index * cut, cut, 0) for index in range(cuts)]]
    swaps = [[]]

    def turn(index, *waits):
        hop = 1 + max(at for at, ring in enumerate(rings) if len(ring) > index)
        value = rings[hop - 1][index]
        if len(rings) == hop:
            rings.append([])
        rings[hop].append(moved(after(value, *waits) if waits else value, "seq", 1))

    def swap(hop, index, *waits):
        value = rings[hop][index]
        if len(swaps) == hop:
            swaps.append([])
        swaps[hop].append([moved(after(value, *waits) if waits else value, "parts", across) for across in range(1, parts)])

    for index in range(cuts):
        turn(index)

    slots = list(project(where, embed, norm_gain[None, :], w_in.transpose(1, 0, 2), seqs, parts))
    later = after(ids, slots[-1])
    near = [ids] + [moved(later, "seq", hop) for hop in range(1, seqs)]
    turned = jnp.stack(near[::-1] + near[::-1])
    every_id = lax.dynamic_slice_in_dim(turned, seqs - 1 - seq, seqs, 0).reshape(1, seqs * held)
    place = lax.broadcasted_iota(jnp.int32, (parts, rows, 1), 1)
    order = lax.broadcasted_iota(jnp.int32, (parts, rows, 1), 0)
    place = place + lax.rem(part - order + parts, parts) * rows
    hot = (place.reshape(vocab, 1) == every_id).astype(jnp.bfloat16)

    bit = 1
    while bit < seqs:
        for slot in range(seqs - bit, 0, -2 * bit):
            got = swapped(slots[slot].astype(jnp.bfloat16), "seq", bit)
            if bit == 1 and slot == seqs - 1:
                got = after(got, *rings[1])
            slots[slot ^ bit] = slots[slot ^ bit].astype(jnp.float32) + got.astype(jnp.float32)
        bit *= 2
    table = slots[0].astype(jnp.bfloat16).reshape(3, mine, rows)
    for index in range(cuts):
        swap(1, index)
    table = after(table, *[one[0] for one in swaps[1]])
    tables = [table] + [moved(table, "parts", across) for across in range(1, parts)]

    first = seq * mine
    short = lax.dynamic_slice_in_dim(short_filter.reshape(3 * SHORT, chans), first, mine, 1)
    skip = lax.dynamic_slice_in_dim(skip_bias, first, mine, 0)
    factors = jnp.concatenate([short, skip[None, :], jnp.zeros((6, mine), jnp.float32)], axis=0).T
    groups = long_filter.shape[0] // seqs
    bands = bands_of(lax.dynamic_slice_in_dim(long_filter, seq * groups, groups, 0))
    cuts = 2
    size = share // cuts
    one = rings[1][0]
    rings[1] = [lax.slice_in_dim(one, index * size, (index + 1) * size, axis=0) for index in range(cuts)]
    for hop in range(2, seqs - 1):
        for index in range(cuts):
            turn(index, *([table] if hop == 2 else []))
    rings[1] = [one]
    sends = mixing(where, tables, hot, factors, bands, seqs)

    sends = list(after(tuple(sends), rings[2][0]))
    for hop in range(2, seqs - 1):
        for index in range(cuts):
            swap(hop, index)
    got = [swapped(sends[hop], "seq", hop) for hop in range(1, seqs)]
    got[0] = after(got[0], *rings[2])
    got[-1] = after(got[-1], swaps[2][0][0])
    for index in range(cuts):
        turn(index, *got)
        swap(seqs - 1, index)
    stack = jnp.concatenate([sends[0]] + got, axis=0)
    stacks = []
    for across in range(fsdps):
        near = stack if across == 0 else moved(stack, "fsdp", across)
        if across:
            near = after(near, swaps[2][1][0])
        stacks += [near] + [moved(near, "chan", turn) for turn in range(1, cores)]

    position = fsdp * cores + core
    onehot = (ids[:, None] == lax.broadcasted_iota(jnp.int32, (1, vocab), 1)).astype(jnp.bfloat16)
    residual = jnp.dot(
        onehot,
        lax.dynamic_slice_in_dim(embed, position * chans, chans, 1),
        preferred_element_type=jnp.float32,
    )
    axes = (parts, seqs, fsdps, cores, depth)
    early, late = [(w_out, (0, 0, 0))], []
    for hop in range(1, seqs):
        size = share // len(rings[hop])
        for index, ring in enumerate(rings[hop]):
            early.append((ring, (hop, 0, index * size)))
            for across in range(1, parts):
                last = hop == seqs - 1 and index == len(rings[hop]) - 1
                (late if last else early).append((swaps[hop][index][across - 1], (hop, across, index * size)))
    begun = output(axes, where, residual, stacks, *zip(*early), jnp.float32 if late else jnp.bfloat16)
    if not late:
        return begun
    return output(axes, where, begun, stacks, *zip(*late), jnp.bfloat16)


def solution(mesh):
    in_specs = (
        P(("parts", "seq")),
        P(),
        P(),
        P("seq", None, ("fsdp", "chan")),
        P(None, None, ("fsdp", "chan")),
        P(("fsdp", "chan"), None),
        P(("fsdp", "chan")),
        P("seq", ("fsdp", "chan")),
    )
    out_specs = P(("parts", "seq"), ("fsdp", "chan"))
    return jax.shard_map(
        on_device, mesh=mesh, in_specs=in_specs, out_specs=out_specs, check_vma=False
    )
```

```python
import functools

import jax
import jax.numpy as jnp
from jax import lax
from jax.experimental import pallas as pl
from jax.experimental.pallas import tpu as pltpu
from jax.sharding import PartitionSpec as P

FL = 128
SHORT = 3
VMEM = 28 * 1024 * 1024


def moved(value, axis, steps):
    count = lax.axis_size(axis)
    return lax.ppermute(value, axis, [(source, (source + steps) % count) for source in range(count)])


def swapped(value, axis, bits):
    count = lax.axis_size(axis)
    return lax.ppermute(value, axis, [(source, source ^ bits) for source in range(count)])


def after(value, *others):
    return lax.optimization_barrier((value,) + others)[0]


def project_kernel(where, rows, cut, gain, w, *refs):
    outs, (normed, turned) = refs[:-2], refs[-2:]
    seqs = len(outs)
    mine = outs[0].shape[0] // 3
    branch = pl.program_id(0)

    @pl.when(branch == 0)
    def _():
        values = rows[...].astype(jnp.float32)
        scale = lax.rsqrt(jnp.mean(values * values, axis=1, keepdims=True) + 1e-06)
        normed[...] = (cut[...].astype(jnp.float32) * scale * gain[...]).astype(jnp.bfloat16)

    turned[...] = jnp.dot(normed[...], w[0], preferred_element_type=jnp.float32).T
    for slot in range(seqs):
        dest = where[1] ^ slot
        piece = turned[pl.ds(pl.multiple_of(dest * mine, mine), mine), :]
        outs[slot][pl.ds(pl.multiple_of(branch * mine, mine), mine), :] = piece.astype(outs[slot].dtype)


def project(where, embed, gain, w, seqs, parts):
    branches, depth, chans = w.shape
    rows = embed.shape[0] // parts
    mine = chans // seqs
    width = embed.shape[1]
    kinds = [jnp.float32] + [jnp.bfloat16] * (seqs - 1)
    return pl.pallas_call(
        project_kernel,
        grid_spec=pltpu.PrefetchScalarGridSpec(
            num_scalar_prefetch=1,
            grid=(branches,),
            in_specs=[
                pl.BlockSpec((rows, width), lambda i, at: (at[0], 0)),
                pl.BlockSpec((rows, depth), lambda i, at: (at[0], at[1])),
                pl.BlockSpec((1, depth), lambda i, at: (0, at[1])),
                pl.BlockSpec((1, depth, chans), lambda i, at: (i, 0, 0)),
            ],
            out_specs=[pl.BlockSpec((branches * mine, rows), lambda i, at: (0, 0))] * seqs,
            scratch_shapes=[pltpu.VMEM((rows, depth), jnp.bfloat16), pltpu.VMEM((chans, rows), jnp.float32)],
        ),
        out_shape=[jax.ShapeDtypeStruct((branches * mine, rows), kind) for kind in kinds],
        compiler_params=pltpu.CompilerParams(vmem_limit_bytes=VMEM),
        cost_estimate=pl.CostEstimate(
            flops=2 * rows * depth * chans * branches,
            bytes_accessed=2 * (rows * width + depth * chans * branches),
            transcendentals=0,
        ),
    )(where, embed, embed, gain, w)


def bands_kernel(taps, out):
    groups = taps.shape[0]
    for group in range(groups):
        line = jnp.concatenate([taps[group : group + 1, :], jnp.zeros((1, FL), jnp.float32)], axis=1)
        wide = jnp.broadcast_to(line, (2 * FL, 2 * FL))
        band = pltpu.roll(wide, FL, 1, stride=1, stride_axis=0)[:, :FL]
        high = band.astype(jnp.bfloat16)
        low = (band - high.astype(jnp.float32)).astype(jnp.bfloat16)
        out[group] = jnp.concatenate([high, low], axis=1)


def bands_of(taps):
    groups = taps.shape[0]
    return pl.pallas_call(
        bands_kernel,
        out_shape=jax.ShapeDtypeStruct((groups, 2 * FL, 2 * FL), jnp.bfloat16),
        compiler_params=pltpu.CompilerParams(vmem_limit_bytes=VMEM),
    )(taps)


def mixing_kernel(per_group, parts, where, *refs):
    tables, (hot, factors, bands), rest = refs[:parts], refs[parts : parts + 3], refs[parts + 3 :]
    outs, (wide, gated) = rest[:-2], rest[-2:]
    seqs = len(outs)
    lanes, held = outs[0].shape
    tokens = hot.shape[1]
    blocks = tokens // FL
    rows = tables[0].shape[2]
    for branch in range(3):
        total = None
        for piece in range(parts):
            term = jnp.dot(
                tables[piece][branch],
                hot[piece * rows : (piece + 1) * rows, :],
                preferred_element_type=jnp.float32,
            )
            total = term if total is None else total + term
        wide[branch] = total
    place = lax.broadcasted_iota(jnp.int32, (per_group, tokens), 1)
    for group in range(lanes // per_group):
        at = slice(group * per_group, (group + 1) * per_group)

        def mixed(branch):
            now = wide[branch, at, :]
            total = factors[at, branch : branch + 1] * now
            for offset in range(1, SHORT):
                before = jnp.where(place >= offset, pltpu.roll(now, offset, 1), 0.0)
                column = 3 * offset + branch
                total = total + factors[at, column : column + 1] * before
            return total

        product = (mixed(1) * mixed(2)).astype(jnp.bfloat16)
        past = jnp.concatenate([jnp.zeros((per_group, FL), jnp.bfloat16), product[:, :-FL]], axis=1)
        windows = jnp.concatenate(
            [
                jnp.concatenate([past[:, b * FL : (b + 1) * FL], product[:, b * FL : (b + 1) * FL]], axis=1)
                for b in range(blocks)
            ],
            axis=0,
        )
        both = jnp.dot(windows, bands[group], preferred_element_type=jnp.float32)
        summed = both[:, :FL] + both[:, FL:]
        conv = jnp.concatenate([summed[b * per_group : (b + 1) * per_group] for b in range(blocks)], axis=1)
        skip = factors[at, 3 * SHORT : 3 * SHORT + 1]
        gated[at, :] = mixed(0) * (conv + skip * product.astype(jnp.float32))
    for slot in range(seqs):
        dest = where[1] ^ slot
        outs[slot][...] = gated[:, pl.ds(pl.multiple_of(dest * held, FL), held)].astype(jnp.bfloat16)


def mixing(where, tables, hot, factors, bands, seqs):
    _, mine, rows = tables[0].shape
    parts = len(tables)
    tokens = hot.shape[1]
    groups = bands.shape[0]
    per_group = mine // groups
    step = min(mine, FL)
    held = tokens // seqs
    return pl.pallas_call(
        functools.partial(mixing_kernel, per_group, parts),
        grid_spec=pltpu.PrefetchScalarGridSpec(
            num_scalar_prefetch=1,
            grid=(mine // step,),
            in_specs=[pl.BlockSpec((3, step, rows), lambda i, at: (0, i, 0))] * parts
            + [
                pl.BlockSpec(hot.shape, lambda i, at: (0, 0)),
                pl.BlockSpec((step, factors.shape[1]), lambda i, at: (i, 0)),
                pl.BlockSpec((step // per_group, 2 * FL, 2 * FL), lambda i, at: (i, 0, 0)),
            ],
            out_specs=[pl.BlockSpec((step, held), lambda i, at: (i, 0))] * seqs,
            scratch_shapes=[
                pltpu.VMEM((3, step, tokens), jnp.float32),
                pltpu.VMEM((step, tokens), jnp.float32),
            ],
        ),
        out_shape=[jax.ShapeDtypeStruct((mine, held), jnp.bfloat16)] * seqs,
        compiler_params=pltpu.CompilerParams(vmem_limit_bytes=VMEM),
        cost_estimate=pl.CostEstimate(
            flops=2 * 3 * mine * rows * parts * tokens,
            bytes_accessed=2 * hot.size,
            transcendentals=0,
        ),
    )(where, *tables, hot, factors, bands)


def output_kernel(axes, stacks, layout, count, where, *refs):
    parts, seqs, fsdps, cores, depth = axes
    start, arrived, refs = refs[0], refs[1 : 1 + stacks], refs[1 + stacks :]
    pieces, (out, gated, total) = refs[:count], refs[count:]
    part, seq, fsdp, core = where[0], where[1], where[2], where[3]
    chans = total.shape[1]
    mine = chans // seqs
    whole = layout[0][2] is None
    shard = layout[0][1](seq) * depth
    for across in range(fsdps):
        for turn in range(cores):
            block = lax.rem(fsdp - across + fsdps, fsdps) * cores + lax.rem(core - turn + cores, cores)
            for hop in range(seqs):
                row = block * chans + (seq ^ hop) * mine

                def place(row=row, hop=hop, at=across * cores + turn):
                    gated[pl.ds(pl.multiple_of(row, mine), mine), :] = arrived[at][hop * mine : (hop + 1) * mine, :]

                if whole:
                    place()
                else:
                    pl.when((row < shard + depth) & (row + mine > shard))(place)
    for index, (size, owner, across, first, sources) in enumerate(layout):
        row = owner(seq) * depth + first
        if across is not None:
            row = row + lax.rem(part - across + parts, parts) * (depth // parts)
        found = [pieces[at][offset : offset + size, :] for at, offset in sources]
        value = found[0] if len(found) == 1 else jnp.where((seq == 0) | (seq == seqs - 1), found[1], found[0])
        term = lax.dot_general(
            gated[pl.ds(pl.multiple_of(row, size), size), :],
            value,
            (((0,), (0,)), ((), ())),
            preferred_element_type=jnp.float32,
        )
        term = term + (total[...] if index else start[...])
        if index == len(layout) - 1:
            out[...] = term.astype(out.dtype)
        else:
            total[...] = term


def output(axes, where, start, stacks, layout, kind):
    parts, seqs, fsdps, cores, depth = axes
    held, chans = start.shape
    pieces, entries = [], []
    for size, owner, across, first, sources in layout:
        spots = []
        for array, offset in sources:
            if not any(array is piece for piece in pieces):
                pieces.append(array)
            spots.append(([array is piece for piece in pieces].index(True), offset))
        entries.append((size, owner, across, first, tuple(spots)))
    size = sum(entry[0] for entry in entries)
    local = pl.BlockSpec(memory_space=pltpu.VMEM)
    return pl.pallas_call(
        functools.partial(output_kernel, axes, len(stacks), tuple(entries), len(pieces)),
        in_specs=[pl.BlockSpec(memory_space=pltpu.SMEM)] + [local] * (1 + len(stacks) + len(pieces)),
        out_specs=local,
        scratch_shapes=[
            pltpu.VMEM((seqs * depth, held), jnp.bfloat16),
            pltpu.VMEM((held, chans), jnp.float32),
        ],
        out_shape=jax.ShapeDtypeStruct((held, chans), kind),
        compiler_params=pltpu.CompilerParams(vmem_limit_bytes=VMEM),
        cost_estimate=pl.CostEstimate(
            flops=2 * held * size * chans, bytes_accessed=2 * size * chans, transcendentals=0
        ),
    )(where, start, *stacks, *pieces)


def on_device(ids, embed, norm_gain, w_in, short_filter, long_filter, skip_bias, w_out):
    held = ids.shape[0]
    chans = skip_bias.shape[0]
    vocab = embed.shape[0]
    seqs, parts = lax.axis_size("seq"), lax.axis_size("parts")
    fsdps, cores = lax.axis_size("fsdp"), lax.axis_size("chan")
    seq, part = lax.axis_index("seq"), lax.axis_index("parts")
    fsdp, core = lax.axis_index("fsdp"), lax.axis_index("chan")
    mine = chans // seqs
    rows = vocab // parts
    depth = w_out.shape[0]
    share = depth // parts
    where = jnp.stack([part, seq, fsdp, core]).astype(jnp.int32)
    line = seqs == 4

    def along(value, pairs):
        return lax.ppermute(value, "seq", pairs)

    def swap(value, planes=None):
        if planes is None:
            return moved(value, "parts", 1)
        pairs = [(p * seqs + s, (p + 1) % parts * seqs + s) for p in range(parts) for s in planes]
        return lax.ppermute(value, ("parts", "seq"), pairs)

    share_of = lax.dynamic_slice_in_dim(w_out, part * share, share, 0)
    layout = [(depth, lambda s: s, None, 0, [(w_out, 0)])]
    last = []
    inner, outer, middle, outward = (1, 2), (0, 3), [(1, 2), (2, 1)], [(1, 0), (2, 3)]
    if line:
        first_near = along(share_of, [(s, s ^ 1) for s in range(seqs)])
        first_mid = along(share_of, middle)
    else:
        ring, nears = share_of, []
        for hop in range(1, seqs):
            ring = moved(ring, "seq", 1)
            nears.append((ring, swap(ring)))

    slots = list(project(where, embed, norm_gain[None, :], w_in.transpose(1, 0, 2), seqs, parts))
    later = after(ids, slots[-1])
    near = [ids] + [moved(later, "seq", hop) for hop in range(1, seqs)]
    turned = jnp.stack(near[::-1] + near[::-1])
    every_id = lax.dynamic_slice_in_dim(turned, seqs - 1 - seq, seqs, 0).reshape(1, seqs * held)
    place = lax.broadcasted_iota(jnp.int32, (parts, rows, 1), 1)
    order = lax.broadcasted_iota(jnp.int32, (parts, rows, 1), 0)
    place = place + lax.rem(part - order + parts, parts) * rows
    hot = (place.reshape(vocab, 1) == every_id).astype(jnp.bfloat16)
    bit = 1
    while bit < seqs:
        for slot in range(seqs - bit, 0, -2 * bit):
            got = swapped(slots[slot].astype(jnp.bfloat16), "seq", bit)
            if line and bit == 1 and slot == seqs - 1:
                got = after(got, first_near, first_mid, *near[1:])
                pass
            slots[slot ^ bit] = slots[slot ^ bit].astype(jnp.float32) + got.astype(jnp.float32)
        bit *= 2
        if line and bit == 2:
            pass
    table = slots[0].astype(jnp.bfloat16).reshape(3, mine, rows)
    if line:
        near_y = swap(first_near)
        table = after(table, near_y)
    tables = [table] + [moved(table, "parts", across) for across in range(1, parts)]
    if line:
        pass
        cross = along(after(first_near, table), middle)
        out_second = along(after(first_mid, table), outward)
        mid_y = swap(after(first_mid, tables[1]), inner)

    first = seq * mine
    short = lax.dynamic_slice_in_dim(short_filter.reshape(3 * SHORT, chans), first, mine, 1)
    skip = lax.dynamic_slice_in_dim(skip_bias, first, mine, 0)
    factors = jnp.concatenate([short, skip[None, :], jnp.zeros((6, mine), jnp.float32)], axis=0).T
    groups = long_filter.shape[0] // seqs
    bands = bands_of(lax.dynamic_slice_in_dim(long_filter, seq * groups, groups, 0))
    sends = mixing(where, tables, hot, factors, bands, seqs)
    if line:
        pass
        second_y = swap(out_second, outer)
        cross_y = swap(cross, inner)

    got = [swapped(sends[hop], "seq", hop) for hop in range(1, seqs)]
    if line:
        pass
        got[0] = after(got[0], out_second, cross)
        pieces = [lax.slice_in_dim(cross, i * (share // 1), (i + 1) * (share // 1), axis=0) for i in range(1)] if 1 > 1 else [cross]
        out_third = [along(after(piece, got[0]), outward) for piece in pieces]
        third_y = [swap(piece, outer) for piece in out_third]
    stack = jnp.concatenate([sends[0]] + got, axis=0)
    stacks = []
    for across in range(fsdps):
        near = stack if across == 0 else moved(stack, "fsdp", across)
        if line and across:
            pass
            near = after(near, second_y, cross_y, mid_y, *out_third)
        stacks += [near] + [moved(near, "chan", turn) for turn in range(1, cores)]

    position = fsdp * cores + core
    onehot = (ids[:, None] == lax.broadcasted_iota(jnp.int32, (1, vocab), 1)).astype(jnp.bfloat16)
    residual = jnp.dot(
        onehot,
        lax.dynamic_slice_in_dim(embed, position * chans, chans, 1),
        preferred_element_type=jnp.float32,
    )
    axes = (parts, seqs, fsdps, cores, depth)
    if line:
        second = lambda s: jnp.where(s < 2, 2, 1)
        third = lambda s: jnp.where(s < 2, 3, 0)
        layout += [(share, lambda s: s ^ 1, 0, 0, [(first_near, 0)]), (share, lambda s: s ^ 1, 1, 0, [(near_y, 0)])]
        layout += [(share, second, 0, 0, [(first_mid, 0), (out_second, 0)]), (share, second, 1, 0, [(mid_y, 0), (second_y, 0)])]
        size = share // len(out_third)
        for index, (piece, piece_y) in enumerate(zip(out_third, third_y)):
            layout.append((size, third, 0, index * size, [(cross, index * size), (piece, 0)]))
            (last if index == len(out_third) - 1 else layout).append((size, third, 1, index * size, [(cross_y, index * size), (piece_y, 0)]))
        pass
    else:
        for hop, (one, other) in enumerate(nears, 1):
            owner = functools.partial(lambda hop, s: lax.rem(s - hop + seqs, seqs), hop)
            layout += [(share, owner, 0, 0, [(one, 0)]), (share, owner, 1, 0, [(other, 0)])]
    begun = output(axes, where, residual, stacks, layout, jnp.float32 if last else jnp.bfloat16)
    if not last:
        return begun
    return output(axes, where, begun, stacks, last, jnp.bfloat16)


def solution(mesh):
    in_specs = (
        P(("parts", "seq")),
        P(),
        P(),
        P("seq", None, ("fsdp", "chan")),
        P(None, None, ("fsdp", "chan")),
        P(("fsdp", "chan"), None),
        P(("fsdp", "chan")),
        P("seq", ("fsdp", "chan")),
    )
    out_specs = P(("parts", "seq"), ("fsdp", "chan"))
    return jax.shard_map(
        on_device, mesh=mesh, in_specs=in_specs, out_specs=out_specs, check_vma=False
    )
```

```python
import functools

import jax
import jax.numpy as jnp
from jax import lax
from jax.experimental import pallas as pl
from jax.experimental.pallas import tpu as pltpu
from jax.sharding import PartitionSpec as P

FL = 128
SHORT = 3
VMEM = 28 * 1024 * 1024


def moved(value, axis, steps):
    count = lax.axis_size(axis)
    return lax.ppermute(value, axis, [(source, (source + steps) % count) for source in range(count)])


def swapped(value, axis, bits):
    count = lax.axis_size(axis)
    return lax.ppermute(value, axis, [(source, source ^ bits) for source in range(count)])


def after(value, *others):
    return lax.optimization_barrier((value,) + others)[0]


def project_kernel(where, rows, cut, gain, w, *refs):
    outs, (normed, turned) = refs[:-2], refs[-2:]
    seqs = len(outs)
    mine = outs[0].shape[0] // 3
    branch = pl.program_id(0)

    @pl.when(branch == 0)
    def _():
        values = rows[...].astype(jnp.float32)
        scale = lax.rsqrt(jnp.mean(values * values, axis=1, keepdims=True) + 1e-06)
        normed[...] = (cut[...].astype(jnp.float32) * scale * gain[...]).astype(jnp.bfloat16)

    turned[...] = jnp.dot(normed[...], w[0], preferred_element_type=jnp.float32).T
    for slot in range(seqs):
        dest = where[1] ^ slot
        piece = turned[pl.ds(pl.multiple_of(dest * mine, mine), mine), :]
        outs[slot][pl.ds(pl.multiple_of(branch * mine, mine), mine), :] = piece.astype(outs[slot].dtype)


def project(where, embed, gain, w, seqs, parts):
    branches, depth, chans = w.shape
    rows = embed.shape[0] // parts
    mine = chans // seqs
    width = embed.shape[1]
    kinds = [jnp.float32] + [jnp.bfloat16] * (seqs - 1)
    return pl.pallas_call(
        project_kernel,
        grid_spec=pltpu.PrefetchScalarGridSpec(
            num_scalar_prefetch=1,
            grid=(branches,),
            in_specs=[
                pl.BlockSpec((rows, width), lambda i, at: (at[0], 0)),
                pl.BlockSpec((rows, depth), lambda i, at: (at[0], at[1])),
                pl.BlockSpec((1, depth), lambda i, at: (0, at[1])),
                pl.BlockSpec((1, depth, chans), lambda i, at: (i, 0, 0)),
            ],
            out_specs=[pl.BlockSpec((branches * mine, rows), lambda i, at: (0, 0))] * seqs,
            scratch_shapes=[pltpu.VMEM((rows, depth), jnp.bfloat16), pltpu.VMEM((chans, rows), jnp.float32)],
        ),
        out_shape=[jax.ShapeDtypeStruct((branches * mine, rows), kind) for kind in kinds],
        compiler_params=pltpu.CompilerParams(vmem_limit_bytes=VMEM),
        cost_estimate=pl.CostEstimate(
            flops=2 * rows * depth * chans * branches,
            bytes_accessed=2 * (rows * width + depth * chans * branches),
            transcendentals=0,
        ),
    )(where, embed, embed, gain, w)


def bands_kernel(taps, out):
    groups = taps.shape[0]
    for group in range(groups):
        line = jnp.concatenate([taps[group : group + 1, :], jnp.zeros((1, FL), jnp.float32)], axis=1)
        wide = jnp.broadcast_to(line, (2 * FL, 2 * FL))
        band = pltpu.roll(wide, FL, 1, stride=1, stride_axis=0)[:, :FL]
        high = band.astype(jnp.bfloat16)
        low = (band - high.astype(jnp.float32)).astype(jnp.bfloat16)
        out[group] = jnp.concatenate([high, low], axis=1)


def bands_of(taps):
    groups = taps.shape[0]
    return pl.pallas_call(
        bands_kernel,
        out_shape=jax.ShapeDtypeStruct((groups, 2 * FL, 2 * FL), jnp.bfloat16),
        compiler_params=pltpu.CompilerParams(vmem_limit_bytes=VMEM),
    )(taps)


def mixing_kernel(per_group, parts, where, *refs):
    tables, (hot, factors, bands), rest = refs[:parts], refs[parts : parts + 3], refs[parts + 3 :]
    outs, (wide, gated) = rest[:-2], rest[-2:]
    seqs = len(outs)
    lanes, held = outs[0].shape
    tokens = hot.shape[1]
    blocks = tokens // FL
    rows = tables[0].shape[2]
    for branch in range(3):
        total = None
        for piece in range(parts):
            term = jnp.dot(
                tables[piece][branch],
                hot[piece * rows : (piece + 1) * rows, :],
                preferred_element_type=jnp.float32,
            )
            total = term if total is None else total + term
        wide[branch] = total
    place = lax.broadcasted_iota(jnp.int32, (per_group, tokens), 1)
    for group in range(lanes // per_group):
        at = slice(group * per_group, (group + 1) * per_group)

        def mixed(branch):
            now = wide[branch, at, :]
            total = factors[at, branch : branch + 1] * now
            for offset in range(1, SHORT):
                before = jnp.where(place >= offset, pltpu.roll(now, offset, 1), 0.0)
                column = 3 * offset + branch
                total = total + factors[at, column : column + 1] * before
            return total

        product = (mixed(1) * mixed(2)).astype(jnp.bfloat16)
        past = jnp.concatenate([jnp.zeros((per_group, FL), jnp.bfloat16), product[:, :-FL]], axis=1)
        windows = jnp.concatenate(
            [
                jnp.concatenate([past[:, b * FL : (b + 1) * FL], product[:, b * FL : (b + 1) * FL]], axis=1)
                for b in range(blocks)
            ],
            axis=0,
        )
        both = jnp.dot(windows, bands[group], preferred_element_type=jnp.float32)
        summed = both[:, :FL] + both[:, FL:]
        conv = jnp.concatenate([summed[b * per_group : (b + 1) * per_group] for b in range(blocks)], axis=1)
        skip = factors[at, 3 * SHORT : 3 * SHORT + 1]
        gated[at, :] = mixed(0) * (conv + skip * product.astype(jnp.float32))
    for slot in range(seqs):
        dest = where[1] ^ slot
        outs[slot][...] = gated[:, pl.ds(pl.multiple_of(dest * held, FL), held)].astype(jnp.bfloat16)


def mixing(where, tables, hot, factors, bands, seqs):
    _, mine, rows = tables[0].shape
    parts = len(tables)
    tokens = hot.shape[1]
    groups = bands.shape[0]
    per_group = mine // groups
    step = min(mine, FL)
    held = tokens // seqs
    return pl.pallas_call(
        functools.partial(mixing_kernel, per_group, parts),
        grid_spec=pltpu.PrefetchScalarGridSpec(
            num_scalar_prefetch=1,
            grid=(mine // step,),
            in_specs=[pl.BlockSpec((3, step, rows), lambda i, at: (0, i, 0))] * parts
            + [
                pl.BlockSpec(hot.shape, lambda i, at: (0, 0)),
                pl.BlockSpec((step, factors.shape[1]), lambda i, at: (i, 0)),
                pl.BlockSpec((step // per_group, 2 * FL, 2 * FL), lambda i, at: (i, 0, 0)),
            ],
            out_specs=[pl.BlockSpec((step, held), lambda i, at: (i, 0))] * seqs,
            scratch_shapes=[
                pltpu.VMEM((3, step, tokens), jnp.float32),
                pltpu.VMEM((step, tokens), jnp.float32),
            ],
        ),
        out_shape=[jax.ShapeDtypeStruct((mine, held), jnp.bfloat16)] * seqs,
        compiler_params=pltpu.CompilerParams(vmem_limit_bytes=VMEM),
        cost_estimate=pl.CostEstimate(
            flops=2 * 3 * mine * rows * parts * tokens,
            bytes_accessed=2 * hot.size,
            transcendentals=0,
        ),
    )(where, *tables, hot, factors, bands)


def output_kernel(axes, stacks, layout, count, where, *refs):
    parts, seqs, fsdps, cores, depth = axes
    start, arrived, refs = refs[0], refs[1 : 1 + stacks], refs[1 + stacks :]
    pieces, (out, gated, total) = refs[:count], refs[count:]
    part, seq, fsdp, core = where[0], where[1], where[2], where[3]
    chans = total.shape[1]
    mine = chans // seqs
    whole = layout[0][2] is None
    shard = layout[0][1](seq) * depth
    for across in range(fsdps):
        for turn in range(cores):
            block = lax.rem(fsdp - across + fsdps, fsdps) * cores + lax.rem(core - turn + cores, cores)
            for hop in range(seqs):
                row = block * chans + (seq ^ hop) * mine

                def place(row=row, hop=hop, at=across * cores + turn):
                    gated[pl.ds(pl.multiple_of(row, mine), mine), :] = arrived[at][hop * mine : (hop + 1) * mine, :]

                if whole:
                    place()
                else:
                    pl.when((row < shard + depth) & (row + mine > shard))(place)
    for index, (size, owner, across, first, sources) in enumerate(layout):
        row = owner(seq) * depth + first
        if across is not None:
            row = row + lax.rem(part - across + parts, parts) * (depth // parts)
        found = [pieces[at][offset : offset + size, :] for at, offset in sources]
        value = found[0] if len(found) == 1 else jnp.where((seq == 0) | (seq == seqs - 1), found[1], found[0])
        term = lax.dot_general(
            gated[pl.ds(pl.multiple_of(row, size), size), :],
            value,
            (((0,), (0,)), ((), ())),
            preferred_element_type=jnp.float32,
        )
        term = term + (total[...] if index else start[...])
        if index == len(layout) - 1:
            out[...] = term.astype(out.dtype)
        else:
            total[...] = term


def output(axes, where, start, stacks, layout, kind):
    parts, seqs, fsdps, cores, depth = axes
    held, chans = start.shape
    pieces, entries = [], []
    for size, owner, across, first, sources in layout:
        spots = []
        for array, offset in sources:
            if not any(array is piece for piece in pieces):
                pieces.append(array)
            spots.append(([array is piece for piece in pieces].index(True), offset))
        entries.append((size, owner, across, first, tuple(spots)))
    size = sum(entry[0] for entry in entries)
    local = pl.BlockSpec(memory_space=pltpu.VMEM)
    return pl.pallas_call(
        functools.partial(output_kernel, axes, len(stacks), tuple(entries), len(pieces)),
        in_specs=[pl.BlockSpec(memory_space=pltpu.SMEM)] + [local] * (1 + len(stacks) + len(pieces)),
        out_specs=local,
        scratch_shapes=[
            pltpu.VMEM((seqs * depth, held), jnp.bfloat16),
            pltpu.VMEM((held, chans), jnp.float32),
        ],
        out_shape=jax.ShapeDtypeStruct((held, chans), kind),
        compiler_params=pltpu.CompilerParams(vmem_limit_bytes=VMEM),
        cost_estimate=pl.CostEstimate(
            flops=2 * held * size * chans, bytes_accessed=2 * size * chans, transcendentals=0
        ),
    )(where, start, *stacks, *pieces)


def on_device(ids, embed, norm_gain, w_in, short_filter, long_filter, skip_bias, w_out):
    held = ids.shape[0]
    chans = skip_bias.shape[0]
    vocab = embed.shape[0]
    seqs, parts = lax.axis_size("seq"), lax.axis_size("parts")
    fsdps, cores = lax.axis_size("fsdp"), lax.axis_size("chan")
    seq, part = lax.axis_index("seq"), lax.axis_index("parts")
    fsdp, core = lax.axis_index("fsdp"), lax.axis_index("chan")
    mine = chans // seqs
    rows = vocab // parts
    depth = w_out.shape[0]
    share = depth // parts
    where = jnp.stack([part, seq, fsdp, core]).astype(jnp.int32)
    line = seqs == 4

    def along(value, pairs):
        return lax.ppermute(value, "seq", pairs)

    def swap(value, planes=None):
        if planes is None:
            return moved(value, "parts", 1)
        pairs = [(p * seqs + s, (p + 1) % parts * seqs + s) for p in range(parts) for s in planes]
        return lax.ppermute(value, ("parts", "seq"), pairs)

    share_of = lax.dynamic_slice_in_dim(w_out, part * share, share, 0)
    layout = [(depth, lambda s: s, None, 0, [(w_out, 0)])]
    last = []
    inner, outer, middle, outward = (1, 2), (0, 3), [(1, 2), (2, 1)], [(1, 0), (2, 3)]
    if line:
        first_near = along(share_of, [(s, s ^ 1) for s in range(seqs)])
        first_mid = along(share_of, middle)
    else:
        ring, nears = share_of, []
        for hop in range(1, seqs):
            ring = moved(ring, "seq", 1)
            nears.append((ring, swap(ring)))

    slots = list(project(where, embed, norm_gain[None, :], w_in.transpose(1, 0, 2), seqs, parts))
    later = after(ids, slots[-1])
    near = [ids] + [moved(later, "seq", hop) for hop in range(1, seqs)]
    turned = jnp.stack(near[::-1] + near[::-1])
    every_id = lax.dynamic_slice_in_dim(turned, seqs - 1 - seq, seqs, 0).reshape(1, seqs * held)
    place = lax.broadcasted_iota(jnp.int32, (parts, rows, 1), 1)
    order = lax.broadcasted_iota(jnp.int32, (parts, rows, 1), 0)
    place = place + lax.rem(part - order + parts, parts) * rows
    hot = (place.reshape(vocab, 1) == every_id).astype(jnp.bfloat16)
    bit = 1
    while bit < seqs:
        for slot in range(seqs - bit, 0, -2 * bit):
            got = swapped(slots[slot].astype(jnp.bfloat16), "seq", bit)
            if line and bit == 1 and slot == seqs - 1:
                got = after(got, first_near, first_mid, *near[1:])
                pass
            slots[slot ^ bit] = slots[slot ^ bit].astype(jnp.float32) + got.astype(jnp.float32)
        bit *= 2
        if line and bit == 2:
            pass
    table = slots[0].astype(jnp.bfloat16).reshape(3, mine, rows)
    if line:
        near_y = swap(first_near)
        table = after(table, near_y)
    tables = [table] + [moved(table, "parts", across) for across in range(1, parts)]
    if line:
        pass
        cross = along(after(first_near, got), middle)
        out_second = along(after(first_mid, got), outward)
        mid_y = swap(after(first_mid, tables[1]), inner)

    first = seq * mine
    short = lax.dynamic_slice_in_dim(short_filter.reshape(3 * SHORT, chans), first, mine, 1)
    skip = lax.dynamic_slice_in_dim(skip_bias, first, mine, 0)
    factors = jnp.concatenate([short, skip[None, :], jnp.zeros((6, mine), jnp.float32)], axis=0).T
    groups = long_filter.shape[0] // seqs
    bands = bands_of(lax.dynamic_slice_in_dim(long_filter, seq * groups, groups, 0))
    sends = mixing(where, tables, hot, factors, bands, seqs)
    if line:
        pass
        second_y = swap(out_second, outer)
        cross_y = swap(cross, inner)

    got = [swapped(sends[hop], "seq", hop) for hop in range(1, seqs)]
    if line:
        pass
        got[0] = after(got[0], out_second, cross)
        pieces = [lax.slice_in_dim(cross, i * (share // 1), (i + 1) * (share // 1), axis=0) for i in range(1)] if 1 > 1 else [cross]
        out_third = [along(after(piece, got[0]), outward) for piece in pieces]
        third_y = [swap(piece, outer) for piece in out_third]
    stack = jnp.concatenate([sends[0]] + got, axis=0)
    stacks = []
    for across in range(fsdps):
        near = stack if across == 0 else moved(stack, "fsdp", across)
        if line and across:
            pass
            near = after(near, second_y, cross_y, mid_y, *out_third)
        stacks += [near] + [moved(near, "chan", turn) for turn in range(1, cores)]

    position = fsdp * cores + core
    onehot = (ids[:, None] == lax.broadcasted_iota(jnp.int32, (1, vocab), 1)).astype(jnp.bfloat16)
    residual = jnp.dot(
        onehot,
        lax.dynamic_slice_in_dim(embed, position * chans, chans, 1),
        preferred_element_type=jnp.float32,
    )
    axes = (parts, seqs, fsdps, cores, depth)
    if line:
        second = lambda s: jnp.where(s < 2, 2, 1)
        third = lambda s: jnp.where(s < 2, 3, 0)
        layout += [(share, lambda s: s ^ 1, 0, 0, [(first_near, 0)]), (share, lambda s: s ^ 1, 1, 0, [(near_y, 0)])]
        layout += [(share, second, 0, 0, [(first_mid, 0), (out_second, 0)]), (share, second, 1, 0, [(mid_y, 0), (second_y, 0)])]
        size = share // len(out_third)
        for index, (piece, piece_y) in enumerate(zip(out_third, third_y)):
            layout.append((size, third, 0, index * size, [(cross, index * size), (piece, 0)]))
            (last if index == len(out_third) - 1 else layout).append((size, third, 1, index * size, [(cross_y, index * size), (piece_y, 0)]))
        pass
    else:
        for hop, (one, other) in enumerate(nears, 1):
            owner = functools.partial(lambda hop, s: lax.rem(s - hop + seqs, seqs), hop)
            layout += [(share, owner, 0, 0, [(one, 0)]), (share, owner, 1, 0, [(other, 0)])]
    begun = output(axes, where, residual, stacks, layout, jnp.float32 if last else jnp.bfloat16)
    if not last:
        return begun
    return output(axes, where, begun, stacks, last, jnp.bfloat16)


def solution(mesh):
    in_specs = (
        P(("parts", "seq")),
        P(),
        P(),
        P("seq", None, ("fsdp", "chan")),
        P(None, None, ("fsdp", "chan")),
        P(("fsdp", "chan"), None),
        P(("fsdp", "chan")),
        P("seq", ("fsdp", "chan")),
    )
    out_specs = P(("parts", "seq"), ("fsdp", "chan"))
    return jax.shard_map(
        on_device, mesh=mesh, in_specs=in_specs, out_specs=out_specs, check_vma=False
    )
```

```python
import functools

import jax
import jax.numpy as jnp
from jax import lax
from jax.experimental import pallas as pl
from jax.experimental.pallas import tpu as pltpu
from jax.sharding import PartitionSpec as P

FL = 128
SHORT = 3
VMEM = 28 * 1024 * 1024


def moved(value, axis, steps):
    count = lax.axis_size(axis)
    return lax.ppermute(value, axis, [(source, (source + steps) % count) for source in range(count)])


def swapped(value, axis, bits):
    count = lax.axis_size(axis)
    return lax.ppermute(value, axis, [(source, source ^ bits) for source in range(count)])


def after(value, *others):
    return lax.optimization_barrier((value,) + others)[0]


def project_kernel(where, rows, cut, gain, w, *refs):
    outs, (normed, turned) = refs[:-2], refs[-2:]
    seqs = len(outs)
    mine = outs[0].shape[0] // 3
    branch = pl.program_id(0)

    @pl.when(branch == 0)
    def _():
        values = rows[...].astype(jnp.float32)
        scale = lax.rsqrt(jnp.mean(values * values, axis=1, keepdims=True) + 1e-06)
        normed[...] = (cut[...].astype(jnp.float32) * scale * gain[...]).astype(jnp.bfloat16)

    turned[...] = jnp.dot(normed[...], w[0], preferred_element_type=jnp.float32).T
    for slot in range(seqs):
        dest = where[1] ^ slot
        piece = turned[pl.ds(pl.multiple_of(dest * mine, mine), mine), :]
        outs[slot][pl.ds(pl.multiple_of(branch * mine, mine), mine), :] = piece.astype(outs[slot].dtype)


def project(where, embed, gain, w, seqs, parts):
    branches, depth, chans = w.shape
    rows = embed.shape[0] // parts
    mine = chans // seqs
    width = embed.shape[1]
    kinds = [jnp.float32] + [jnp.bfloat16] * (seqs - 1)
    return pl.pallas_call(
        project_kernel,
        grid_spec=pltpu.PrefetchScalarGridSpec(
            num_scalar_prefetch=1,
            grid=(branches,),
            in_specs=[
                pl.BlockSpec((rows, width), lambda i, at: (at[0], 0)),
                pl.BlockSpec((rows, depth), lambda i, at: (at[0], at[1])),
                pl.BlockSpec((1, depth), lambda i, at: (0, at[1])),
                pl.BlockSpec((1, depth, chans), lambda i, at: (i, 0, 0)),
            ],
            out_specs=[pl.BlockSpec((branches * mine, rows), lambda i, at: (0, 0))] * seqs,
            scratch_shapes=[pltpu.VMEM((rows, depth), jnp.bfloat16), pltpu.VMEM((chans, rows), jnp.float32)],
        ),
        out_shape=[jax.ShapeDtypeStruct((branches * mine, rows), kind) for kind in kinds],
        compiler_params=pltpu.CompilerParams(vmem_limit_bytes=VMEM),
        cost_estimate=pl.CostEstimate(
            flops=2 * rows * depth * chans * branches,
            bytes_accessed=2 * (rows * width + depth * chans * branches),
            transcendentals=0,
        ),
    )(where, embed, embed, gain, w)


def bands_kernel(taps, out):
    groups = taps.shape[0]
    for group in range(groups):
        line = jnp.concatenate([taps[group : group + 1, :], jnp.zeros((1, FL), jnp.float32)], axis=1)
        wide = jnp.broadcast_to(line, (2 * FL, 2 * FL))
        band = pltpu.roll(wide, FL, 1, stride=1, stride_axis=0)[:, :FL]
        high = band.astype(jnp.bfloat16)
        low = (band - high.astype(jnp.float32)).astype(jnp.bfloat16)
        out[group] = jnp.concatenate([high, low], axis=1)


def bands_of(taps):
    groups = taps.shape[0]
    return pl.pallas_call(
        bands_kernel,
        out_shape=jax.ShapeDtypeStruct((groups, 2 * FL, 2 * FL), jnp.bfloat16),
        compiler_params=pltpu.CompilerParams(vmem_limit_bytes=VMEM),
    )(taps)


def mixing_kernel(per_group, parts, where, *refs):
    tables, (hot, factors, bands), rest = refs[:parts], refs[parts : parts + 3], refs[parts + 3 :]
    outs, (wide, gated) = rest[:-2], rest[-2:]
    seqs = len(outs)
    lanes, held = outs[0].shape
    tokens = hot.shape[1]
    blocks = tokens // FL
    rows = tables[0].shape[2]
    for branch in range(3):
        total = None
        for piece in range(parts):
            term = jnp.dot(
                tables[piece][branch],
                hot[piece * rows : (piece + 1) * rows, :],
                preferred_element_type=jnp.float32,
            )
            total = term if total is None else total + term
        wide[branch] = total
    place = lax.broadcasted_iota(jnp.int32, (per_group, tokens), 1)
    for group in range(lanes // per_group):
        at = slice(group * per_group, (group + 1) * per_group)

        def mixed(branch):
            now = wide[branch, at, :]
            total = factors[at, branch : branch + 1] * now
            for offset in range(1, SHORT):
                before = jnp.where(place >= offset, pltpu.roll(now, offset, 1), 0.0)
                column = 3 * offset + branch
                total = total + factors[at, column : column + 1] * before
            return total

        product = (mixed(1) * mixed(2)).astype(jnp.bfloat16)
        past = jnp.concatenate([jnp.zeros((per_group, FL), jnp.bfloat16), product[:, :-FL]], axis=1)
        windows = jnp.concatenate(
            [
                jnp.concatenate([past[:, b * FL : (b + 1) * FL], product[:, b * FL : (b + 1) * FL]], axis=1)
                for b in range(blocks)
            ],
            axis=0,
        )
        both = jnp.dot(windows, bands[group], preferred_element_type=jnp.float32)
        summed = both[:, :FL] + both[:, FL:]
        conv = jnp.concatenate([summed[b * per_group : (b + 1) * per_group] for b in range(blocks)], axis=1)
        skip = factors[at, 3 * SHORT : 3 * SHORT + 1]
        gated[at, :] = mixed(0) * (conv + skip * product.astype(jnp.float32))
    for slot in range(seqs):
        dest = where[1] ^ slot
        outs[slot][...] = gated[:, pl.ds(pl.multiple_of(dest * held, FL), held)].astype(jnp.bfloat16)


def mixing(where, tables, hot, factors, bands, seqs):
    _, mine, rows = tables[0].shape
    parts = len(tables)
    tokens = hot.shape[1]
    groups = bands.shape[0]
    per_group = mine // groups
    step = min(mine, FL)
    held = tokens // seqs
    return pl.pallas_call(
        functools.partial(mixing_kernel, per_group, parts),
        grid_spec=pltpu.PrefetchScalarGridSpec(
            num_scalar_prefetch=1,
            grid=(mine // step,),
            in_specs=[pl.BlockSpec((3, step, rows), lambda i, at: (0, i, 0))] * parts
            + [
                pl.BlockSpec(hot.shape, lambda i, at: (0, 0)),
                pl.BlockSpec((step, factors.shape[1]), lambda i, at: (i, 0)),
                pl.BlockSpec((step // per_group, 2 * FL, 2 * FL), lambda i, at: (i, 0, 0)),
            ],
            out_specs=[pl.BlockSpec((step, held), lambda i, at: (i, 0))] * seqs,
            scratch_shapes=[
                pltpu.VMEM((3, step, tokens), jnp.float32),
                pltpu.VMEM((step, tokens), jnp.float32),
            ],
        ),
        out_shape=[jax.ShapeDtypeStruct((mine, held), jnp.bfloat16)] * seqs,
        compiler_params=pltpu.CompilerParams(vmem_limit_bytes=VMEM),
        cost_estimate=pl.CostEstimate(
            flops=2 * 3 * mine * rows * parts * tokens,
            bytes_accessed=2 * hot.size,
            transcendentals=0,
        ),
    )(where, *tables, hot, factors, bands)


def output_kernel(axes, stacks, layout, count, where, *refs):
    parts, seqs, fsdps, cores, depth = axes
    start, arrived, refs = refs[0], refs[1 : 1 + stacks], refs[1 + stacks :]
    pieces, (out, gated, total) = refs[:count], refs[count:]
    part, seq, fsdp, core = where[0], where[1], where[2], where[3]
    chans = total.shape[1]
    mine = chans // seqs
    whole = layout[0][2] is None
    shard = layout[0][1](seq) * depth
    for across in range(fsdps):
        for turn in range(cores):
            block = lax.rem(fsdp - across + fsdps, fsdps) * cores + lax.rem(core - turn + cores, cores)
            for hop in range(seqs):
                row = block * chans + (seq ^ hop) * mine

                def place(row=row, hop=hop, at=across * cores + turn):
                    gated[pl.ds(pl.multiple_of(row, mine), mine), :] = arrived[at][hop * mine : (hop + 1) * mine, :]

                if whole:
                    place()
                else:
                    pl.when((row < shard + depth) & (row + mine > shard))(place)
    for index, (size, owner, across, first, sources) in enumerate(layout):
        row = owner(seq) * depth + first
        if across is not None:
            row = row + lax.rem(part - across + parts, parts) * (depth // parts)
        found = [pieces[at][offset : offset + size, :] for at, offset in sources]
        value = found[0] if len(found) == 1 else jnp.where((seq == 0) | (seq == seqs - 1), found[1], found[0])
        term = lax.dot_general(
            gated[pl.ds(pl.multiple_of(row, size), size), :],
            value,
            (((0,), (0,)), ((), ())),
            preferred_element_type=jnp.float32,
        )
        term = term + (total[...] if index else start[...])
        if index == len(layout) - 1:
            out[...] = term.astype(out.dtype)
        else:
            total[...] = term


def output(axes, where, start, stacks, layout, kind):
    parts, seqs, fsdps, cores, depth = axes
    held, chans = start.shape
    pieces, entries = [], []
    for size, owner, across, first, sources in layout:
        spots = []
        for array, offset in sources:
            if not any(array is piece for piece in pieces):
                pieces.append(array)
            spots.append(([array is piece for piece in pieces].index(True), offset))
        entries.append((size, owner, across, first, tuple(spots)))
    size = sum(entry[0] for entry in entries)
    local = pl.BlockSpec(memory_space=pltpu.VMEM)
    return pl.pallas_call(
        functools.partial(output_kernel, axes, len(stacks), tuple(entries), len(pieces)),
        in_specs=[pl.BlockSpec(memory_space=pltpu.SMEM)] + [local] * (1 + len(stacks) + len(pieces)),
        out_specs=local,
        scratch_shapes=[
            pltpu.VMEM((seqs * depth, held), jnp.bfloat16),
            pltpu.VMEM((held, chans), jnp.float32),
        ],
        out_shape=jax.ShapeDtypeStruct((held, chans), kind),
        compiler_params=pltpu.CompilerParams(vmem_limit_bytes=VMEM),
        cost_estimate=pl.CostEstimate(
            flops=2 * held * size * chans, bytes_accessed=2 * size * chans, transcendentals=0
        ),
    )(where, start, *stacks, *pieces)


def on_device(ids, embed, norm_gain, w_in, short_filter, long_filter, skip_bias, w_out):
    held = ids.shape[0]
    chans = skip_bias.shape[0]
    vocab = embed.shape[0]
    seqs, parts = lax.axis_size("seq"), lax.axis_size("parts")
    fsdps, cores = lax.axis_size("fsdp"), lax.axis_size("chan")
    seq, part = lax.axis_index("seq"), lax.axis_index("parts")
    fsdp, core = lax.axis_index("fsdp"), lax.axis_index("chan")
    mine = chans // seqs
    rows = vocab // parts
    depth = w_out.shape[0]
    share = depth // parts
    where = jnp.stack([part, seq, fsdp, core]).astype(jnp.int32)
    line = seqs == 4

    def along(value, pairs):
        return lax.ppermute(value, "seq", pairs)

    def swap(value, planes=None):
        if planes is None:
            return moved(value, "parts", 1)
        pairs = [(p * seqs + s, (p + 1) % parts * seqs + s) for p in range(parts) for s in planes]
        return lax.ppermute(value, ("parts", "seq"), pairs)

    share_of = lax.dynamic_slice_in_dim(w_out, part * share, share, 0)
    layout = [(depth, lambda s: s, None, 0, [(w_out, 0)])]
    last = []
    inner, outer, middle, outward = (1, 2), (0, 3), [(1, 2), (2, 1)], [(1, 0), (2, 3)]
    if line:
        first_near = along(share_of, [(s, s ^ 1) for s in range(seqs)])
        first_mid = along(share_of, middle)
    else:
        ring, nears = share_of, []
        for hop in range(1, seqs):
            ring = moved(ring, "seq", 1)
            nears.append((ring, swap(ring)))

    slots = list(project(where, embed, norm_gain[None, :], w_in.transpose(1, 0, 2), seqs, parts))
    later = after(ids, slots[-1])
    near = [ids] + [moved(later, "seq", hop) for hop in range(1, seqs)]
    turned = jnp.stack(near[::-1] + near[::-1])
    every_id = lax.dynamic_slice_in_dim(turned, seqs - 1 - seq, seqs, 0).reshape(1, seqs * held)
    place = lax.broadcasted_iota(jnp.int32, (parts, rows, 1), 1)
    order = lax.broadcasted_iota(jnp.int32, (parts, rows, 1), 0)
    place = place + lax.rem(part - order + parts, parts) * rows
    hot = (place.reshape(vocab, 1) == every_id).astype(jnp.bfloat16)
    bit = 1
    while bit < seqs:
        for slot in range(seqs - bit, 0, -2 * bit):
            got = swapped(slots[slot].astype(jnp.bfloat16), "seq", bit)
            if line and bit == 1 and slot == seqs - 1:
                got = after(got, first_near, first_mid, *near[1:])
                pass
            slots[slot ^ bit] = slots[slot ^ bit].astype(jnp.float32) + got.astype(jnp.float32)
        bit *= 2
        if line and bit == 2:
            pass
            out_second = along(after(first_mid, got), outward)
    table = slots[0].astype(jnp.bfloat16).reshape(3, mine, rows)
    if line:
        near_y = swap(first_near)
        table = after(table, near_y)
    tables = [table] + [moved(table, "parts", across) for across in range(1, parts)]
    if line:
        pass
        cross = along(after(first_near, got), middle)
        mid_y = swap(after(first_mid, tables[1]), inner)

    first = seq * mine
    short = lax.dynamic_slice_in_dim(short_filter.reshape(3 * SHORT, chans), first, mine, 1)
    skip = lax.dynamic_slice_in_dim(skip_bias, first, mine, 0)
    factors = jnp.concatenate([short, skip[None, :], jnp.zeros((6, mine), jnp.float32)], axis=0).T
    groups = long_filter.shape[0] // seqs
    bands = bands_of(lax.dynamic_slice_in_dim(long_filter, seq * groups, groups, 0))
    sends = mixing(where, tables, hot, factors, bands, seqs)
    if line:
        pass
        second_y = swap(out_second, outer)
        cross_y = swap(cross, inner)

    got = [swapped(sends[hop], "seq", hop) for hop in range(1, seqs)]
    if line:
        pass
        got[0] = after(got[0], cross)
        pieces = [lax.slice_in_dim(cross, i * (share // 1), (i + 1) * (share // 1), axis=0) for i in range(1)] if 1 > 1 else [cross]
        out_third = [along(after(piece, got[0]), outward) for piece in pieces]
        third_y = [swap(piece, outer) for piece in out_third]
    stack = jnp.concatenate([sends[0]] + got, axis=0)
    stacks = []
    for across in range(fsdps):
        near = stack if across == 0 else moved(stack, "fsdp", across)
        if line and across:
            pass
            near = after(near, second_y, cross_y, mid_y, *out_third)
        stacks += [near] + [moved(near, "chan", turn) for turn in range(1, cores)]

    position = fsdp * cores + core
    onehot = (ids[:, None] == lax.broadcasted_iota(jnp.int32, (1, vocab), 1)).astype(jnp.bfloat16)
    residual = jnp.dot(
        onehot,
        lax.dynamic_slice_in_dim(embed, position * chans, chans, 1),
        preferred_element_type=jnp.float32,
    )
    axes = (parts, seqs, fsdps, cores, depth)
    if line:
        second = lambda s: jnp.where(s < 2, 2, 1)
        third = lambda s: jnp.where(s < 2, 3, 0)
        layout += [(share, lambda s: s ^ 1, 0, 0, [(first_near, 0)]), (share, lambda s: s ^ 1, 1, 0, [(near_y, 0)])]
        layout += [(share, second, 0, 0, [(first_mid, 0), (out_second, 0)]), (share, second, 1, 0, [(mid_y, 0), (second_y, 0)])]
        size = share // len(out_third)
        for index, (piece, piece_y) in enumerate(zip(out_third, third_y)):
            layout.append((size, third, 0, index * size, [(cross, index * size), (piece, 0)]))
            (last if index == len(out_third) - 1 else layout).append((size, third, 1, index * size, [(cross_y, index * size), (piece_y, 0)]))
        pass
    else:
        for hop, (one, other) in enumerate(nears, 1):
            owner = functools.partial(lambda hop, s: lax.rem(s - hop + seqs, seqs), hop)
            layout += [(share, owner, 0, 0, [(one, 0)]), (share, owner, 1, 0, [(other, 0)])]
    begun = output(axes, where, residual, stacks, layout, jnp.float32 if last else jnp.bfloat16)
    if not last:
        return begun
    return output(axes, where, begun, stacks, last, jnp.bfloat16)


def solution(mesh):
    in_specs = (
        P(("parts", "seq")),
        P(),
        P(),
        P("seq", None, ("fsdp", "chan")),
        P(None, None, ("fsdp", "chan")),
        P(("fsdp", "chan"), None),
        P(("fsdp", "chan")),
        P("seq", ("fsdp", "chan")),
    )
    out_specs = P(("parts", "seq"), ("fsdp", "chan"))
    return jax.shard_map(
        on_device, mesh=mesh, in_specs=in_specs, out_specs=out_specs, check_vma=False
    )
```
